32 devices in a mesh: groups: 2 (over y), tm: 4 (over z), space: 2 (over x), pair: 2 (over core).
Axes of the slice: x: 2, y: 2, z: 4, core: 2. Of those that a mesh axis runs over, the one named last changes fastest.
Arguments:
- link_field: float32 [4, 4, 16, 16, 4, 256], P(None, None, 'tm', 'space', 'pair', 'groups'), parts along dimension 5, may hold values from -1 to 1, as said below
Outputs:
- rotated_links: float32 [3, 4, 16, 16, 4, 256], P(None, None, 'tm', 'space', 'pair', 'groups'), parts along dimension 5
The draws below stay inside these ranges and needn't reach their ends.
There are 2 independent parts, one for each index of `groups`. The reference program is written for one: setup_inputs(seed, part) draws one part's arguments, and reference() takes and returns one part's arrays. A program takes and returns all parts, laid end to end along the dimension named above; each array names one. Nothing has to cross between parts.
Inputs may be any that keep to these rules, and one draw needn't show every extreme that they name: `link_field`: every link is a unit quaternion: its four components' squares sum to one.
All inputs are finite; a program needn't handle non-finite values.
Results may differ from the reference program's by a relative error of at most 0.0001.
Values sent between devices are 32-bit elements; how exact they have to be, the bound alone decides.
No kernel may reach another device: no remote copies, remote signals or barrier semaphores. Data moves between devices by JAX's collectives and lax.ppermute only.
A program may use at most 64 MiB of HBM per device.

```python
import jax
import jax.numpy as jnp
from jax import lax

Z = 128
SWEEPS = 2
TT = 16
LX = 16
LY = 4


def draw_link_field(key, part):
    sample = jax.random.normal(key, (4, 4, TT, LX, LY, Z), jnp.float32)
    return sample / jnp.sqrt(jnp.sum(sample * sample, axis=1, keepdims=True))


def setup_inputs(seed: int = 0, part: int = 0) -> dict:
    streams_of = jax.random.split(jax.random.key(seed), 2)
    part_keys = jax.random.split(jax.random.fold_in(streams_of[1], part), 2)
    return {
        "link_field": draw_link_field(jax.random.fold_in(jax.random.fold_in(streams_of[1], part), 71), part),
    }


smear_weight = 0.1

def quat_mul(former, latter):
    return jnp.stack([former[0] * latter[0] - former[1] * latter[1] - former[2] * latter[2] - former[3] * latter[3], former[0] * latter[1] + former[1] * latter[0] + former[2] * latter[3] - former[3] * latter[2], former[0] * latter[2] - former[1] * latter[3] + former[2] * latter[0] + former[3] * latter[1], former[0] * latter[3] + former[1] * latter[2] - former[2] * latter[1] + former[3] * latter[0]])

def quat_conj(quat_field):
    return jnp.concatenate([quat_field[:1], -quat_field[1:]], axis=0)

def unit_step(direction):
    return tuple((1 if slot == direction else 0 for slot in range(4)))

def shifted(quat_field, offset):
    cropped = quat_field[:, 1 + offset[0]:quat_field.shape[1] - 1 + offset[0], 1 + offset[1]:quat_field.shape[2] - 1 + offset[1], 1 + offset[2]:quat_field.shape[3] - 1 + offset[2], :]
    if offset[3] != 0:
        cropped = jnp.roll(cropped, -offset[3], axis=-1)
    return cropped

def smear_padded(padded):
    anchor = (0, 0, 0, 0)
    results = []
    for lead_dir in range(4):
        current = shifted(padded[lead_dir], anchor)
        staple_sum = jnp.zeros_like(current)
        forward = unit_step(lead_dir)
        for side_dir in range(4):
            if side_dir == lead_dir:
                continue
            across = unit_step(side_dir)
            backward = tuple((-value for value in across))
            diagonal = tuple((backward[slot] + forward[slot] for slot in range(4)))
            upper_path = quat_mul(quat_mul(shifted(padded[side_dir], anchor), shifted(padded[lead_dir], across)), quat_conj(shifted(padded[side_dir], forward)))
            lower_path = quat_mul(quat_mul(quat_conj(shifted(padded[side_dir], backward)), shifted(padded[lead_dir], backward)), shifted(padded[side_dir], diagonal))
            staple_sum = staple_sum + upper_path + lower_path
        combined = current + smear_weight * staple_sum
        results.append(combined / jnp.sqrt(lax.optimization_barrier(jnp.sum(combined * combined, axis=0, keepdims=True))))
    return jnp.stack(results)

def reference(link_field):
    smeared = link_field
    for sweep_index in range(SWEEPS):
        padded = jnp.pad(smeared, ((0, 0), (0, 0), (1, 1), (1, 1), (1, 1), (0, 0)), mode='wrap')
        smeared = smear_padded(padded)
    temporal = smeared[0]
    first_slice = temporal[:, 0]
    identity = jnp.concatenate([jnp.ones_like(first_slice[:1]), jnp.zeros_like(first_slice[1:])], axis=0)

    def advance(carry_in, link_slice):
        return (quat_mul(carry_in, link_slice), carry_in)
    unused, prefixes = lax.scan(advance, identity, jnp.moveaxis(temporal, 1, 0))
    gauge_field = jnp.moveaxis(prefixes, 0, 1)
    rotated = []
    for spatial in range(1, 4):
        neighbour = jnp.roll(gauge_field, -1, axis=spatial + 1)
        rotated.append(quat_mul(quat_mul(gauge_field, smeared[spatial]), quat_conj(neighbour)))
    return jnp.stack(rotated)
```

```python
import jax
import jax.numpy as jnp
from jax import lax
from jax.experimental import pallas as pl
from jax.experimental.pallas import tpu as pltpu
from jax.sharding import PartitionSpec as P

SWEEPS = 2
smear_weight = 0.1
VMEM = pl.BlockSpec(memory_space=pltpu.VMEM)
F32 = jnp.float32
BASE = 8


def mul(a, b):
    return (
        a[0] * b[0] - a[1] * b[1] - a[2] * b[2] - a[3] * b[3],
        a[0] * b[1] + a[1] * b[0] + a[2] * b[3] - a[3] * b[2],
        a[0] * b[2] - a[1] * b[3] + a[2] * b[0] + a[3] * b[1],
        a[0] * b[3] + a[1] * b[2] - a[2] * b[1] + a[3] * b[0],
    )


def mul_cr(a, b):
    return (
        a[0] * b[0] + a[1] * b[1] + a[2] * b[2] + a[3] * b[3],
        a[1] * b[0] - a[0] * b[1] - a[2] * b[3] + a[3] * b[2],
        a[2] * b[0] - a[0] * b[2] + a[1] * b[3] - a[3] * b[1],
        a[3] * b[0] - a[0] * b[3] - a[1] * b[2] + a[2] * b[1],
    )


def mul_cl(a, b):
    return (
        a[0] * b[0] + a[1] * b[1] + a[2] * b[2] + a[3] * b[3],
        a[0] * b[1] - a[1] * b[0] - a[2] * b[3] + a[3] * b[2],
        a[0] * b[2] + a[1] * b[3] - a[2] * b[0] - a[3] * b[1],
        a[0] * b[3] - a[1] * b[2] + a[2] * b[1] - a[3] * b[0],
    )


def add(a, b):
    return tuple(x + y for x, y in zip(a, b))


def zroll(a, amount):
    return tuple(pltpu.roll(x, amount % 128, 1) for x in a)


def fill_scratch(own, par, t_below, t_above, xh, corner, t_shared, x_shared, eo, ep):
    tl = own.shape[2]
    for d in range(4):
        eo[d, :, 1 : tl + 1, BASE : BASE + 16, :] = own[d]
        ep[d, :, 1 : tl + 1, BASE : BASE + 16, :] = par[d]
    eo[:, :, 0, BASE : BASE + 16, :] = t_below[...]
    eo[1:4, :, tl + 1, BASE : BASE + 16, :] = t_above[...]
    for slot, d in enumerate((0, 2, 3)):
        eo[d, :, 1 : tl + 1, BASE + 16 : BASE + 18, :] = xh[slot]
    for d in range(4):
        eo[d, :, 1 : tl + 1, BASE - 2 : BASE, :] = xh[3 + d]
    ep[0, :, 0, BASE : BASE + 16, :] = t_shared[0]
    ep[2, :, tl + 1, BASE : BASE + 16, :] = t_shared[1]
    ep[2, :, 1 : tl + 1, BASE + 16 : BASE + 18, :] = x_shared[0]
    ep[1, :, 1 : tl + 1, BASE - 2 : BASE, :] = x_shared[1]
    eo[0, :, 0, BASE + 16 : BASE + 18, :] = corner[0]
    eo[1, :, tl + 1, BASE - 2 : BASE, :] = corner[1]


def smear_site(eo, ep, t, y):
    def ld(d, dt=0, dx=0, dy=0):
        yy = y + dy
        ref = eo if 0 <= yy < 2 else ep
        start = BASE + 2 * dx + yy % 2
        return tuple(ref[d, c, t + 1 + dt, pl.ds(start, 8, stride=2), :] for c in range(4))

    def step(m):
        return {0: dict(dt=1), 1: dict(dx=1), 2: dict(dy=1)}[m]

    def back(n):
        return {0: dict(dt=-1), 1: dict(dx=-1), 2: dict(dy=-1)}[n]

    total = [None] * 4

    def acc(m, q):
        total[m] = q if total[m] is None else add(total[m], q)

    here = [ld(d) for d in range(4)]
    for m in range(3):
        for n in range(m + 1, 3):
            um, un = here[m], here[n]
            um_n = ld(m, **step(n))
            un_m = ld(n, **step(m))
            acc(m, mul_cr(mul(un, um_n), un_m))
            acc(n, mul_cr(mul(um, un_m), um_n))
            acc(m, mul(mul_cl(ld(n, **back(n)), ld(m, **back(n))), ld(n, **back(n), **step(m))))
            acc(n, mul(mul_cl(ld(m, **back(m)), ld(n, **back(m))), ld(m, **back(m), **step(n))))
    uz = here[3]
    for m in range(3):
        um = here[m]
        um_z = zroll(um, -1)
        uz_m = ld(3, **step(m))
        a = mul(um, uz_m)
        acc(m, mul_cr(mul(uz, um_z), uz_m))
        acc(3, mul_cr(a, um_z))
        acc(m, zroll(mul_cl(uz, a), 1))
        low = ld(m, **back(m))
        acc(3, mul(mul_cl(low, ld(3, **back(m))), zroll(low, -1)))
    out = []
    for m in range(4):
        comb = tuple(h + smear_weight * s for h, s in zip(here[m], total[m]))
        norm = comb[0] * comb[0] + comb[1] * comb[1] + comb[2] * comb[2] + comb[3] * comb[3]
        inv = lax.rsqrt(norm)
        out.append(tuple(x * inv for x in comb))
    return out


def boundary(out, t_up, t_dn, xs):
    tl = out.shape[2]
    t_up[...] = out[:, :, tl - 1]
    t_dn[...] = out[1:4, :, 0]
    for slot, d in enumerate((0, 2, 3)):
        xs[slot] = out[d, :, :, 0:2, :]
    for d in range(4):
        xs[3 + d] = out[d, :, :, 14:16, :]


def sweep_kernel(own, par, t_below, t_above, xh, corner, t_shared, x_shared, out, t_up, t_dn, xs, eo, ep):
    tl = own.shape[2]
    fill_scratch(own, par, t_below, t_above, xh, corner, t_shared, x_shared, eo, ep)

    def body(t, carry):
        for y in range(2):
            new = smear_site(eo, ep, t, y)
            for d in range(4):
                for c in range(4):
                    out[d, c, t, pl.ds(y, 8, stride=2), :] = new[d][c]
        return carry

    lax.fori_loop(0, tl, body, 0)
    boundary(out, t_up, t_dn, xs)


def last_kernel(own, par, t_below, t_above, xh, corner, t_shared, x_shared, out, prefix, slab, eo, ep):
    tl = own.shape[2]
    fill_scratch(own, par, t_below, t_above, xh, corner, t_shared, x_shared, eo, ep)

    def body(t, carry):
        new_carry = []
        for y in range(2):
            rows = pl.ds(y, 8, stride=2)
            new = smear_site(eo, ep, t, y)
            for d in range(1, 4):
                for c in range(4):
                    out[d - 1, c, t, rows, :] = new[d][c]
            for c in range(4):
                prefix[c, t, rows, :] = carry[y][c]
            new_carry.append(mul(carry[y], new[0]))
        return tuple(new_carry)

    one = jnp.ones((8, 128), F32)
    zero = jnp.zeros((8, 128), F32)
    ident = (one, zero, zero, zero)
    final = lax.fori_loop(0, tl, body, (ident, ident))
    for y in range(2):
        for c in range(4):
            slab[c, pl.ds(y, 8, stride=2), :] = final[y][c]


def carry_kernel(n, prefix, slab_list, gauge, gx, gy):
    tl = prefix.shape[1]
    place = lax.axis_index("tm")
    for half in range(2):
        rows = pl.ds(half * 8, 8)
        state = None
        for j in reversed(range(n - 1)):
            q = tuple(slab_list[j][c, rows, :] for c in range(4))
            there = place >= j + 1
            q = tuple(jnp.where(there, v, 1.0 if c == 0 else 0.0) for c, v in enumerate(q))
            state = q if state is None else mul(state, q)
        for t in range(tl):
            g = mul(state, tuple(prefix[c, t, rows, :] for c in range(4)))
            for c in range(4):
                gauge[c, t, rows, :] = g[c]
    gx[...] = gauge[:, :, 0:2, :]
    for c in range(4):
        for t in range(tl):
            gy[c, t] = gauge[c, t, pl.ds(0, 8, stride=2), :]


def rotate_kernel(gauge, nx, ny, links, out, ext):
    tl = gauge.shape[1]
    ext[:, :, 0:16, :] = gauge[...]
    ext[:, :, 16:18, :] = nx[...]
    for t in range(tl):
        for y in range(2):
            rows = pl.ds(y, 8, stride=2)
            g = tuple(gauge[c, t, rows, :] for c in range(4))
            g1 = tuple(ext[c, t, pl.ds(2 + y, 8, stride=2), :] for c in range(4))
            if y == 0:
                g2 = tuple(gauge[c, t, pl.ds(1, 8, stride=2), :] for c in range(4))
            else:
                g2 = tuple(ny[c, t] for c in range(4))
            g3 = zroll(g, -1)
            for d, other in enumerate((g1, g2, g3)):
                u = tuple(links[d, c, t, rows, :] for c in range(4))
                r = mul_cr(mul(g, u), other)
                for c in range(4):
                    out[d, c, t, rows, :] = r[c]


def call(kernel, outs, scratch, *args):
    single = isinstance(outs[0], int)
    shapes = [jax.ShapeDtypeStruct(s, F32) for s in ([outs] if single else outs)]
    return pl.pallas_call(
        kernel,
        out_shape=shapes[0] if single else shapes,
        in_specs=[VMEM] * len(args),
        out_specs=VMEM if single else [VMEM] * len(shapes),
        scratch_shapes=[pltpu.VMEM(s, F32) for s in scratch],
        compiler_params=pltpu.CompilerParams(vmem_limit_bytes=40 * 2**20),
    )(*args)


def rotated_by(x, axis, steps):
    n = lax.axis_size(axis)
    return lax.ppermute(x, axis, [(i, (i + steps) % n) for i in range(n)])


def x_exchange(xs, cut):
    if lax.axis_size("space") == 2:
        return rotated_by(xs, "space", 1)
    return jnp.concatenate(
        [rotated_by(xs[:cut], "space", -1), rotated_by(xs[cut:], "space", 1)]
    )


def halo(own, t_up, t_dn, xs):
    t_below = rotated_by(t_up, "tm", 1)
    t_above = rotated_by(t_dn, "tm", -1)
    xh = x_exchange(xs, 3)
    par = rotated_by(own, "pair", 1)
    x_shared = rotated_by(jnp.stack([xh[1], xh[4]]), "pair", 1)
    corner = x_exchange(jnp.stack([t_below[0, :, :2], t_above[0, :, -2:]]), 1)
    t_shared = rotated_by(jnp.stack([t_below[0], t_above[1]]), "pair", 1)
    return par, t_below, t_above, xh, corner, t_shared, x_shared


def on_device(link_field):
    tl, xl, yl, z = link_field.shape[2:]
    rows = xl * yl
    links = link_field.reshape(4, 4, tl, rows, z)
    scratch = [(4, 4, tl + 2, 32, z)] * 2
    edges = [(4, 4, rows, z), (3, 4, rows, z), (7, 4, tl, 2, z)]
    t_up, t_dn, xs = call(boundary, edges, [], links)
    for _ in range(SWEEPS - 1):
        got = halo(links, t_up, t_dn, xs)
        links, t_up, t_dn, xs = call(
            sweep_kernel,
            [(4, 4, tl, rows, z)] + edges,
            scratch,
            links,
            *got,
        )
    got = halo(links, t_up, t_dn, xs)
    smeared, prefix, slab = call(
        last_kernel, [(3, 4, tl, rows, z), (4, tl, rows, z), (4, rows, z)], scratch, links, *got
    )
    n = lax.axis_size("tm")
    slabs = [rotated_by(slab, "tm", k) for k in range(1, n)]
    gauge, gx, gy = call(
        lambda p, *rest: carry_kernel(n, p, rest[: n - 1], *rest[n - 1 :]),
        [(4, tl, rows, z), (4, tl, 2, z), (4, tl, xl, z)],
        [],
        prefix,
        *slabs,
    )
    nx = rotated_by(gx, "space", -1)
    ny = rotated_by(gy, "pair", -1)
    out = call(
        rotate_kernel, (3, 4, tl, rows, z), [(4, tl, 24, z)], gauge, nx, ny, smeared
    )
    return out.reshape(3, 4, tl, xl, yl, z)


def solution(mesh):
    spec = P(None, None, "tm", "space", "pair", "groups")
    return jax.shard_map(on_device, mesh=mesh, in_specs=(spec,), out_specs=spec, check_vma=False)
```

```python
import jax
import jax.numpy as jnp
from jax import lax
from jax.experimental import pallas as pl
from jax.experimental.pallas import tpu as pltpu
from jax.sharding import PartitionSpec as P

smear_weight = 0.1
VMEM = pl.BlockSpec(memory_space=pltpu.VMEM)
F32 = jnp.float32
BASE = 8


def mul(a, b):
    return (
        a[0] * b[0] - a[1] * b[1] - a[2] * b[2] - a[3] * b[3],
        a[0] * b[1] + a[1] * b[0] + a[2] * b[3] - a[3] * b[2],
        a[0] * b[2] - a[1] * b[3] + a[2] * b[0] + a[3] * b[1],
        a[0] * b[3] + a[1] * b[2] - a[2] * b[1] + a[3] * b[0],
    )


def mul_cr(a, b):
    return (
        a[0] * b[0] + a[1] * b[1] + a[2] * b[2] + a[3] * b[3],
        a[1] * b[0] - a[0] * b[1] - a[2] * b[3] + a[3] * b[2],
        a[2] * b[0] - a[0] * b[2] + a[1] * b[3] - a[3] * b[1],
        a[3] * b[0] - a[0] * b[3] - a[1] * b[2] + a[2] * b[1],
    )


def mul_cl(a, b):
    return (
        a[0] * b[0] + a[1] * b[1] + a[2] * b[2] + a[3] * b[3],
        a[0] * b[1] - a[1] * b[0] - a[2] * b[3] + a[3] * b[2],
        a[0] * b[2] + a[1] * b[3] - a[2] * b[0] - a[3] * b[1],
        a[0] * b[3] - a[1] * b[2] + a[2] * b[1] - a[3] * b[0],
    )


def add(a, b):
    return tuple(x + y for x, y in zip(a, b))


def zroll(a, amount):
    return tuple(pltpu.roll(x, amount % 128, 1) for x in a)


def accessor(eo, ep, low, high):
    tl = eo.shape[2]
    cache = {}

    def ld(d, t, x, y, z=0):
        key = (d, t, x, y, z)
        if key not in cache:
            if z:
                cache[key] = zroll(ld(d, t, x, y), -z)
            else:
                mine = 0 <= y < 2
                rows = pl.ds(BASE + 2 * x + y % 2, 8, stride=2)
                if 0 <= t < tl:
                    ref = eo if mine else ep
                    cache[key] = tuple(ref[d, c, t, rows, :] for c in range(4))
                else:
                    ref = (low if t < 0 else high)[0 if mine else 1]
                    cache[key] = tuple(ref[d, c, rows, :] for c in range(4))
        return cache[key]

    return ld


def moved(s, d, k=1):
    return tuple(v + k if i == d else v for i, v in enumerate(s))


def smear_link(ld, m, s):
    total = None
    here = ld(m, *s)
    for n in range(4):
        if n == m:
            continue
        u = mul_cr(mul(ld(n, *s), ld(m, *moved(s, n))), ld(n, *moved(s, m)))
        if n == 3:
            v = zroll(mul(mul_cl(ld(n, *s), here), ld(n, *moved(s, m))), 1)
        else:
            b = moved(s, n, -1)
            v = mul(mul_cl(ld(n, *b), ld(m, *b)), ld(n, *moved(b, m)))
        total = add(u, v) if total is None else add(total, add(u, v))
    comb = tuple(h + smear_weight * w for h, w in zip(here, total))
    norm = comb[0] * comb[0] + comb[1] * comb[1] + comb[2] * comb[2] + comb[3] * comb[3]
    inv = lax.rsqrt(norm)
    return tuple(v * inv for v in comb)


def fill(own, par, xh, x_shared, eo, ep):
    for d in range(4):
        eo[d, :, :, BASE : BASE + 16, :] = own[d]
        ep[d, :, :, BASE : BASE + 16, :] = par[d]
        eo[d, :, :, BASE - 2 : BASE, :] = xh[3 + d]
    for slot, d in enumerate((0, 2, 3)):
        eo[d, :, :, BASE + 16 : BASE + 18, :] = xh[slot]
    ep[2, :, :, BASE + 16 : BASE + 18, :] = x_shared[0]
    ep[1, :, :, BASE - 2 : BASE, :] = x_shared[1]
    ep[2, :, :, BASE - 2 : BASE, :] = x_shared[2]


def interior_1(own, par, xh, x_shared, eo, ep, new):
    tl = own.shape[2]
    fill(own, par, xh, x_shared, eo, ep)
    for t in range(1, tl - 1):
        for y in range(2):
            ld = accessor(eo, ep, None, None)
            for d in range(4):
                q = smear_link(ld, d, (t, 0, y, 0))
                for c in range(4):
                    new[d, c, t, pl.ds(y, 8, stride=2), :] = q[c]


MAIN = slice(BASE, BASE + 16)
BEFORE = slice(BASE - 2, BASE)
AFTER = slice(BASE + 16, BASE + 18)


def edges_1(
    eo, ep, part, t_below, t_above, t_shared, corner, new, t_dn, t_up, xs, lo, lp, ho, hp
):
    tl = eo.shape[2]
    lo[:, :, MAIN, :] = t_below[...]
    lo[0, :, AFTER, :] = corner[0]
    lo[0:2, :, BEFORE, :] = corner[2:4]
    lp[0, :, MAIN, :] = t_shared[0]
    lp[2, :, MAIN, :] = t_shared[1]
    ho[1:4, :, MAIN, :] = t_above[...]
    ho[1, :, BEFORE, :] = corner[1]
    hp[2, :, MAIN, :] = t_shared[2]
    for t in range(1, tl - 1):
        new[:, :, t] = part[:, :, t]
    for t in (0, tl - 1):
        for y in range(2):
            ld = accessor(eo, ep, (lo, lp), (ho, hp))
            for d in range(4):
                q = smear_link(ld, d, (t, 0, y, 0))
                for c in range(4):
                    new[d, c, t, pl.ds(y, 8, stride=2), :] = q[c]
    for d in range(3):
        for c in range(4):
            t_dn[64 * d + 16 * c : 64 * d + 16 * c + 16, :] = new[d + 1, c, 0]
    q = smear_link(accessor(eo, ep, (lo, lp), None), 2, (0, 0, -1, 0))
    for c in range(4):
        t_dn[192 + 8 * c : 200 + 8 * c, :] = q[c]
    for y in range(2):
        q = smear_link(accessor(eo, ep, (lo, lp), None), 1, (0, -1, y, 0))
        for c in range(4):
            t_dn[224 + 2 * c + y : 225 + 2 * c + y, :] = q[c][0:1]
    t_up[...] = new[:, :, tl - 1]
    for slot, d in enumerate((0, 2, 3)):
        xs[slot] = new[d, :, :, 0:2, :]
    for d in range(4):
        xs[3 + d] = new[d, :, :, 14:16, :]


def interior_2(own, par, xh, x_shared, eo, ep, prefix, new):
    tl = own.shape[2]
    fill(own, par, xh, x_shared, eo, ep)
    for y in range(2):
        rows = pl.ds(y, 8, stride=2)
        one = jnp.ones((8, 128), F32)
        zero = jnp.zeros((8, 128), F32)
        state = (one, zero, zero, zero)
        for t in range(tl):
            for c in range(4):
                prefix[c, t, rows, :] = state[c]
            if t < tl - 1:
                ld = accessor(eo, ep, None, None)
                q = smear_link(ld, 0, (t, 0, y, 0))
                state = q if t == 0 else mul(state, q)
                if t > 0:
                    for d in range(1, 4):
                        q = smear_link(ld, d, (t, 0, y, 0))
                        for c in range(4):
                            new[d - 1, c, t, rows, :] = q[c]


def slab_kernel(eo, ep, t_above, prefix, slab, ho, hp):
    tl = eo.shape[2]
    for d in range(3):
        for c in range(4):
            ho[d + 1, c, MAIN, :] = t_above[64 * d + 16 * c : 64 * d + 16 * c + 16, :]
    for c in range(4):
        hp[2, c, pl.ds(BASE + 1, 8, stride=2), :] = t_above[192 + 8 * c : 200 + 8 * c, :]
        ho[1, c, BEFORE, :] = t_above[224 + 2 * c : 226 + 2 * c, :]
    for y in range(2):
        rows = pl.ds(y, 8, stride=2)
        q = smear_link(accessor(eo, ep, None, (ho, hp)), 0, (tl - 1, 0, y, 0))
        state = mul(tuple(prefix[c, tl - 1, rows, :] for c in range(4)), q)
        for c in range(4):
            slab[c, rows, :] = state[c]


def edges_2(eo, ep, part, t_above, t_below, t_shared, corner, new, lo, lp, ho):
    tl = eo.shape[2]
    lo[:, :, MAIN, :] = t_below[...]
    lo[0, :, AFTER, :] = corner[...]
    lp[0, :, MAIN, :] = t_shared[...]
    for d in range(3):
        for c in range(4):
            ho[d + 1, c, MAIN, :] = t_above[64 * d + 16 * c : 64 * d + 16 * c + 16, :]
    for t in range(1, tl - 1):
        new[:, :, t] = part[:, :, t]
    for t in (0, tl - 1):
        for y in range(2):
            ld = accessor(eo, ep, (lo, lp), (ho, None))
            for d in range(1, 4):
                q = smear_link(ld, d, (t, 0, y, 0))
                for c in range(4):
                    new[d - 1, c, t, pl.ds(y, 8, stride=2), :] = q[c]


def boundary(out, t_up, t_dn, xs):
    tl = out.shape[2]
    t_up[...] = out[:, :, tl - 1]
    t_dn[...] = out[1:4, :, 0]
    for slot, d in enumerate((0, 2, 3)):
        xs[slot] = out[d, :, :, 0:2, :]
    for d in range(4):
        xs[3 + d] = out[d, :, :, 14:16, :]


def carry_kernel(n, prefix, slab_list, gauge, gx, gy):
    tl = prefix.shape[1]
    place = lax.axis_index("tm")
    for half in range(2):
        rows = pl.ds(half * 8, 8)
        state = None
        for j in reversed(range(n - 1)):
            q = tuple(slab_list[j][c, rows, :] for c in range(4))
            there = place >= j + 1
            q = tuple(jnp.where(there, v, 1.0 if c == 0 else 0.0) for c, v in enumerate(q))
            state = q if state is None else mul(state, q)
        for t in range(tl):
            g = mul(state, tuple(prefix[c, t, rows, :] for c in range(4)))
            for c in range(4):
                gauge[c, t, rows, :] = g[c]
    gx[...] = gauge[:, :, 0:2, :]
    for c in range(4):
        for t in range(tl):
            gy[c, t] = gauge[c, t, pl.ds(0, 8, stride=2), :]


def rotate_kernel(gauge, nx, ny, links, out, ext):
    tl = gauge.shape[1]
    ext[:, :, 0:16, :] = gauge[...]
    ext[:, :, 16:18, :] = nx[...]
    for t in range(tl):
        for y in range(2):
            rows = pl.ds(y, 8, stride=2)
            g = tuple(gauge[c, t, rows, :] for c in range(4))
            g1 = tuple(ext[c, t, pl.ds(2 + y, 8, stride=2), :] for c in range(4))
            if y == 0:
                g2 = tuple(gauge[c, t, pl.ds(1, 8, stride=2), :] for c in range(4))
            else:
                g2 = tuple(ny[c, t] for c in range(4))
            g3 = zroll(g, -1)
            for d, other in enumerate((g1, g2, g3)):
                u = tuple(links[d, c, t, rows, :] for c in range(4))
                r = mul_cr(mul(g, u), other)
                for c in range(4):
                    out[d, c, t, rows, :] = r[c]


def call(kernel, outs, scratch, *args):
    single = isinstance(outs[0], int)
    shapes = [jax.ShapeDtypeStruct(s, F32) for s in ([outs] if single else outs)]
    return pl.pallas_call(
        kernel,
        out_shape=shapes[0] if single else shapes,
        in_specs=[VMEM] * len(args),
        out_specs=VMEM if single else [VMEM] * len(shapes),
        scratch_shapes=[pltpu.VMEM(s, F32) for s in scratch],
        compiler_params=pltpu.CompilerParams(vmem_limit_bytes=40 * 2**20),
    )(*args)


def rotated_by(x, axis, steps):
    n = lax.axis_size(axis)
    return lax.ppermute(x, axis, [(i, (i + steps) % n) for i in range(n)])


def x_exchange(xs, cut):
    if lax.axis_size("space") == 2:
        return rotated_by(xs, "space", 1)
    return jnp.concatenate(
        [rotated_by(xs[:cut], "space", -1), rotated_by(xs[cut:], "space", 1)]
    )


def side_halo(own, xs):
    xh = x_exchange(xs, 3)
    par = rotated_by(own, "pair", 1)
    x_shared = rotated_by(jnp.stack([xh[1], xh[4], xh[5]]), "pair", 1)
    return par, xh, x_shared


def on_device(link_field):
    tl, xl, yl, z = link_field.shape[2:]
    rows = xl * yl
    links = link_field.reshape(4, 4, tl, rows, z)
    block = (4, 4, tl, rows, z)
    ext = (4, 4, tl, 32, z)
    layer = (4, 4, 32, z)
    t_up, t_dn, xs = call(
        boundary, [(4, 4, rows, z), (3, 4, rows, z), (7, 4, tl, 2, z)], [], links
    )
    t_below = rotated_by(t_up, "tm", 1)
    t_above = rotated_by(t_dn, "tm", -1)
    sides = side_halo(links, xs)
    eo, ep, part = call(interior_1, [ext, ext, block], [], links, *sides)
    corner = x_exchange(
        jnp.stack([t_below[0, :, :2], t_above[0, :, -2:], t_below[0, :, -2:], t_below[1, :, -2:]]),
        1,
    )
    t_shared = rotated_by(jnp.stack([t_below[0], t_below[2], t_above[1]]), "pair", 1)
    links, t_dn, t_up, xs = call(
        edges_1,
        [block, (232, z), (4, 4, rows, z), (7, 4, tl, 2, z)],
        [layer] * 4,
        eo,
        ep,
        part,
        t_below,
        t_above,
        t_shared,
        corner,
    )
    t_above = rotated_by(t_dn, "tm", -1)
    t_below = rotated_by(t_up, "tm", 1)
    sides = side_halo(links, xs)
    spatial = (3, 4, tl, rows, z)
    eo, ep, prefix, part = call(
        interior_2, [ext, ext, (4, tl, rows, z), spatial], [], links, *sides
    )
    slab = call(slab_kernel, (4, rows, z), [layer] * 2, eo, ep, t_above, prefix)
    n = lax.axis_size("tm")
    slabs = [rotated_by(slab, "tm", k) for k in range(1, n)]
    corner = rotated_by(t_below[0, :, :2], "space", -1)
    t_shared = rotated_by(t_below[0], "pair", 1)
    smeared = call(
        edges_2, spatial, [layer] * 3, eo, ep, part, t_above, t_below, t_shared, corner
    )
    gauge, gx, gy = call(
        lambda p, *rest: carry_kernel(n, p, rest[: n - 1], *rest[n - 1 :]),
        [(4, tl, rows, z), (4, tl, 2, z), (4, tl, xl, z)],
        [],
        prefix,
        *slabs,
    )
    nx = rotated_by(gx, "space", -1)
    ny = rotated_by(gy, "pair", -1)
    out = call(rotate_kernel, spatial, [(4, tl, 24, z)], gauge, nx, ny, smeared)
    return out.reshape(3, 4, tl, xl, yl, z)


def solution(mesh):
    spec = P(None, None, "tm", "space", "pair", "groups")
    return jax.shard_map(on_device, mesh=mesh, in_specs=(spec,), out_specs=spec, check_vma=False)
```

```python
import jax
import jax.numpy as jnp
from jax import lax
from jax.experimental import pallas as pl
from jax.experimental.pallas import tpu as pltpu
from jax.sharding import PartitionSpec as P

smear_weight = 0.1
LONG = 20_000_000_000
VMEM = pl.BlockSpec(memory_space=pltpu.VMEM)
F32 = jnp.float32
BASE = 8


def mul(a, b):
    return (
        a[0] * b[0] - a[1] * b[1] - a[2] * b[2] - a[3] * b[3],
        a[0] * b[1] + a[1] * b[0] + a[2] * b[3] - a[3] * b[2],
        a[0] * b[2] - a[1] * b[3] + a[2] * b[0] + a[3] * b[1],
        a[0] * b[3] + a[1] * b[2] - a[2] * b[1] + a[3] * b[0],
    )


def mul_cr(a, b):
    return (
        a[0] * b[0] + a[1] * b[1] + a[2] * b[2] + a[3] * b[3],
        a[1] * b[0] - a[0] * b[1] - a[2] * b[3] + a[3] * b[2],
        a[2] * b[0] - a[0] * b[2] + a[1] * b[3] - a[3] * b[1],
        a[3] * b[0] - a[0] * b[3] - a[1] * b[2] + a[2] * b[1],
    )


def mul_cl(a, b):
    return (
        a[0] * b[0] + a[1] * b[1] + a[2] * b[2] + a[3] * b[3],
        a[0] * b[1] - a[1] * b[0] - a[2] * b[3] + a[3] * b[2],
        a[0] * b[2] + a[1] * b[3] - a[2] * b[0] - a[3] * b[1],
        a[0] * b[3] - a[1] * b[2] + a[2] * b[1] - a[3] * b[0],
    )


def add(a, b):
    return tuple(x + y for x, y in zip(a, b))


def zroll(a, amount):
    return tuple(pltpu.roll(x, amount % 128, 1) for x in a)


def accessor(eo, ep, low, high):
    tl = eo.shape[2]
    cache = {}

    def ld(d, t, x, y, z=0):
        key = (d, t, x, y, z)
        if key not in cache:
            if z:
                cache[key] = zroll(ld(d, t, x, y), -z)
            else:
                mine = 0 <= y < 2
                rows = pl.ds(BASE + 2 * x + y % 2, 8, stride=2)
                if 0 <= t < tl:
                    ref = eo if mine else ep
                    cache[key] = tuple(ref[d, c, t, rows, :] for c in range(4))
                else:
                    ref = (low if t < 0 else high)[0 if mine else 1]
                    cache[key] = tuple(ref[d, c, rows, :] for c in range(4))
        return cache[key]

    return ld


def moved(s, d, k=1):
    return tuple(v + k if i == d else v for i, v in enumerate(s))


def lower(ld, m, n, s):
    b = moved(s, n, -1)
    return mul(mul_cl(ld(n, *b), ld(m, *b)), ld(n, *moved(b, m)))


def unit(q):
    norm = q[0] * q[0] + q[1] * q[1] + q[2] * q[2] + q[3] * q[3]
    inv = lax.rsqrt(norm)
    return tuple(v * inv for v in q)


def scaled_add(a, b):
    return tuple(h + smear_weight * w for h, w in zip(a, b))


def combined(ld, m, s, leave=None):
    total = None
    here = ld(m, *s)
    for n in range(4):
        if n == m:
            continue
        u = mul_cr(mul(ld(n, *s), ld(m, *moved(s, n))), ld(n, *moved(s, m)))
        total = u if total is None else add(total, u)
        if n == 3:
            v = zroll(mul(mul_cl(ld(n, *s), here), ld(n, *moved(s, m))), 1)
            total = add(total, v)
        elif n != leave:
            total = add(total, lower(ld, m, n, s))
    return scaled_add(here, total)


def smear_link(ld, m, s):
    return unit(combined(ld, m, s))


def fill(own, par, xh, x_shared, eo, ep):
    for d in range(4):
        eo[d, :, :, BASE : BASE + 16, :] = own[d]
        ep[d, :, :, BASE : BASE + 16, :] = par[d]
        eo[d, :, :, BASE - 2 : BASE, :] = xh[3 + d]
    for slot, d in enumerate((0, 2, 3)):
        eo[d, :, :, BASE + 16 : BASE + 18, :] = xh[slot]
    if x_shared is not None:
        ep[2, :, :, BASE + 16 : BASE + 18, :] = x_shared[0]
        ep[1, :, :, BASE - 2 : BASE, :] = x_shared[1]
        if x_shared.shape[0] > 2:
            ep[2, :, :, BASE - 2 : BASE, :] = x_shared[2]


def interior_1(own, par, xh, x_shared, eo, ep, new):
    tl = own.shape[2]
    fill(own, par, xh, x_shared, eo, ep)
    for t in range(1, tl - 1):
        for y in range(2):
            ld = accessor(eo, ep, None, None)
            for d in range(4):
                q = smear_link(ld, d, (t, 0, y, 0))
                for c in range(4):
                    new[d, c, t, pl.ds(y, 8, stride=2), :] = q[c]


MAIN = slice(BASE, BASE + 16)
BEFORE = slice(BASE - 2, BASE)
AFTER = slice(BASE + 16, BASE + 18)


def first_1(eo, ep, t_below, t_shared, corner, t_dn, first, lo, lp):
    lo[:, :, MAIN, :] = t_below[...]
    lo[0, :, AFTER, :] = corner[0]
    lo[0:2, :, BEFORE, :] = corner[2:4]
    lp[0, :, MAIN, :] = t_shared[0]
    lp[2, :, MAIN, :] = t_shared[1]
    for y in range(2):
        ld = accessor(eo, ep, (lo, lp), None)
        for d in range(4):
            q = smear_link(ld, d, (0, 0, y, 0))
            for c in range(4):
                first[d, c, pl.ds(y, 8, stride=2), :] = q[c]
        q = smear_link(accessor(eo, ep, (lo, lp), None), 1, (0, -1, y, 0))
        for c in range(4):
            t_dn[224 + 2 * c + y : 225 + 2 * c + y, :] = q[c][0:1]
    q = smear_link(accessor(eo, ep, (lo, lp), None), 2, (0, 0, -1, 0))
    for c in range(4):
        t_dn[192 + 8 * c : 200 + 8 * c, :] = q[c]
    for d in range(3):
        for c in range(4):
            t_dn[64 * d + 16 * c : 64 * d + 16 * c + 16, :] = first[d + 1, c]


def rest_1(eo, ep, part, first, t_above, t_shared, corner, new, xs, ho, hp):
    tl = eo.shape[2]
    ho[1:4, :, MAIN, :] = t_above[...]
    ho[1, :, BEFORE, :] = corner[1]
    hp[2, :, MAIN, :] = t_shared[2]
    new[:, :, 0] = first[...]
    for t in range(1, tl - 1):
        new[:, :, t] = part[:, :, t]
    t = tl - 1
    for y in range(2):
        ld = accessor(eo, ep, None, (ho, hp))
        for d in range(4):
            q = smear_link(ld, d, (t, 0, y, 0))
            for c in range(4):
                new[d, c, t, pl.ds(y, 8, stride=2), :] = q[c]
    for slot, d in enumerate((0, 2, 3)):
        xs[slot] = new[d, :, :, 0:2, :]
    for d in range(4):
        xs[3 + d] = new[d, :, :, 14:16, :]


def pack_1(t_below, t_above, edges, shared):
    edges[0] = t_below[0, :, 0:2, :]
    edges[1] = t_above[0, :, 14:16, :]
    edges[2:4] = t_below[0:2, :, 14:16, :]
    shared[0] = t_below[0]
    shared[1] = t_below[2]
    shared[2] = t_above[1]


def unpack_above(t_above, ho):
    for d in range(3):
        for c in range(4):
            ho[d + 1, c, MAIN, :] = t_above[64 * d + 16 * c : 64 * d + 16 * c + 16, :]


def above_2(t_above, ho, hp):
    unpack_above(t_above, ho)
    for c in range(4):
        hp[2, c, pl.ds(BASE + 1, 8, stride=2), :] = t_above[192 + 8 * c : 200 + 8 * c, :]
        ho[1, c, BEFORE, :] = t_above[224 + 2 * c : 226 + 2 * c, :]


def temporal_2(own, par, xh, ho, hp, prefix, slab, eo, ep):
    tl = own.shape[2]
    fill(own, par, xh, None, eo, ep)
    for y in range(2):
        rows = pl.ds(y, 8, stride=2)
        one = jnp.ones((8, 128), F32)
        zero = jnp.zeros((8, 128), F32)
        state = (one, zero, zero, zero)
        for t in range(tl):
            for c in range(4):
                prefix[c, t, rows, :] = state[c]
            q = smear_link(accessor(eo, ep, None, (ho, hp)), 0, (t, 0, y, 0))
            state = q if t == 0 else mul(state, q)
        for c in range(4):
            slab[c, rows, :] = state[c]


def spatial_2(own, par, xh, x_shared, t_above, new, lows, eo, ep, ho):
    tl = own.shape[2]
    fill(own, par, xh, x_shared, eo, ep)
    unpack_above(t_above, ho)
    for t in range(tl):
        for y in range(2):
            ld = accessor(eo, ep, None, (ho, None))
            for d in range(1, 4):
                s = (t, 0, y, 0)
                q = combined(ld, d, s, leave=0) if t == 0 else smear_link(ld, d, s)
                for c in range(4):
                    new[d - 1, c, t, pl.ds(y, 8, stride=2), :] = q[c]
    for y in range(2):
        rows = pl.ds(y, 8, stride=2)
        ld = accessor(eo, ep, None, None)
        for d in range(1, 4):
            s = moved((tl - 1, 0, y, 0), 0)
            q = lower(ld, d, 0, s)
            for c in range(4):
                lows[d - 1, c, rows, :] = q[c]


def carry_kernel(n, prefix, slab_list, ready, gauge, gx, gy):
    tl = prefix.shape[1]
    place = lax.axis_index("tm")
    for half in range(2):
        rows = pl.ds(half * 8, 8)
        state = None
        for j in reversed(range(n - 1)):
            q = tuple(slab_list[j][c, rows, :] for c in range(4))
            there = place >= j + 1
            q = tuple(jnp.where(there, v, 1.0 if c == 0 else 0.0) for c, v in enumerate(q))
            state = q if state is None else mul(state, q)
        for t in range(tl):
            g = mul(state, tuple(prefix[c, t, rows, :] for c in range(4)))
            for c in range(4):
                gauge[c, t, rows, :] = g[c]
    gx[...] = gauge[:, :, 0:2, :]
    for c in range(4):
        for t in range(tl):
            gy[c, t] = gauge[c, t, pl.ds(0, 8, stride=2), :]


def rotate_kernel(gauge, nx, ny, links, lows, out, ext):
    tl = gauge.shape[1]
    ext[:, :, 0:16, :] = gauge[...]
    ext[:, :, 16:18, :] = nx[...]
    for t in range(tl):
        for y in range(2):
            rows = pl.ds(y, 8, stride=2)
            g = tuple(gauge[c, t, rows, :] for c in range(4))
            g1 = tuple(ext[c, t, pl.ds(2 + y, 8, stride=2), :] for c in range(4))
            if y == 0:
                g2 = tuple(gauge[c, t, pl.ds(1, 8, stride=2), :] for c in range(4))
            else:
                g2 = tuple(ny[c, t] for c in range(4))
            for d, other in enumerate((g1, g2, zroll(g, -1))):
                u = tuple(links[d, c, t, rows, :] for c in range(4))
                if t == 0:
                    u = unit(scaled_add(u, tuple(lows[d, c, rows, :] for c in range(4))))
                r = mul_cr(mul(g, u), other)
                for c in range(4):
                    out[d, c, t, rows, :] = r[c]


def boundary(links, t_up, t_dn, xs, copy):
    tl = links.shape[2]
    copy[...] = links[...]
    t_up[...] = links[:, :, tl - 1]
    t_dn[...] = links[1:4, :, 0]
    for slot, d in enumerate((0, 2, 3)):
        xs[slot] = links[d, :, :, 0:2, :]
    for d in range(4):
        xs[3 + d] = links[d, :, :, 14:16, :]


def call(kernel, outs, scratch, *args, weight=1):
    single = isinstance(outs[0], int)
    shapes = [jax.ShapeDtypeStruct(s, F32) for s in ([outs] if single else outs)]
    return pl.pallas_call(
        kernel,
        out_shape=shapes[0] if single else shapes,
        in_specs=[VMEM] * len(args),
        out_specs=VMEM if single else [VMEM] * len(shapes),
        scratch_shapes=[pltpu.VMEM(s, F32) for s in scratch],
        cost_estimate=pl.CostEstimate(flops=weight, bytes_accessed=1, transcendentals=0),
        compiler_params=pltpu.CompilerParams(vmem_limit_bytes=40 * 2**20),
    )(*args)


def rotated_by(x, axis, steps):
    n = lax.axis_size(axis)
    return lax.ppermute(x, axis, [(i, (i + steps) % n) for i in range(n)])


def x_exchange(xs, cut):
    if lax.axis_size("space") == 2:
        return rotated_by(xs, "space", 1)
    return jnp.concatenate(
        [rotated_by(xs[:cut], "space", -1), rotated_by(xs[cut:], "space", 1)]
    )


def to_rows(parts):
    return jnp.concatenate([p.reshape(-1, p.shape[-1]) for p in parts])


def after(value, other):
    return lax.optimization_barrier((value, other))[0]


def on_device(link_field):
    tl, xl, yl, z = link_field.shape[2:]
    rows = xl * yl
    links = link_field.reshape(4, 4, tl, rows, z)
    block = (4, 4, tl, rows, z)
    ext = (4, 4, tl, 32, z)
    layer = (4, 4, 32, z)
    t_up, t_dn, xs, links = call(
        boundary, [(4, 4, rows, z), (3, 4, rows, z), (7, 4, tl, 2, z), block], [], links
    )
    t_below = rotated_by(t_up, "tm", 1)
    t_above = rotated_by(t_dn, "tm", -1)
    xh = x_exchange(xs, 3)
    par = rotated_by(links, "pair", 1)
    edges, shared = call(
        pack_1, [(4, 4, yl, z), (3, 4, rows, z)], [], t_below, t_above, weight=LONG
    )
    corner = x_exchange(edges, 1)
    t_shared = rotated_by(shared, "pair", 1)
    x_shared = rotated_by(jnp.stack([xh[1], xh[4], xh[5]]), "pair", 1)
    eo, ep, part = call(interior_1, [ext, ext, block], [], links, par, xh, x_shared)
    t_dn, first = call(
        first_1, [(232, z), (4, 4, rows, z)], [layer] * 2, eo, ep, t_below, t_shared, corner
    )
    links, xs = call(
        rest_1,
        [block, (7, 4, tl, 2, z)],
        [layer] * 2,
        eo,
        ep,
        part,
        first,
        t_above,
        t_shared,
        corner,
    )
    t_above = rotated_by(t_dn, "tm", -1)
    xh = x_exchange(xs, 3)
    par = rotated_by(links, "pair", 1)
    layers = call(above_2, [layer, layer], [], t_above, weight=LONG)
    prefix, slab = call(
        temporal_2,
        [(4, tl, rows, z), (4, rows, z)],
        [ext, ext],
        links,
        par,
        xh,
        *layers,
    )
    n = lax.axis_size("tm")
    slabs = [rotated_by(slab, "tm", k) for k in range(1, n)]
    x_shared = rotated_by(after(jnp.stack([xh[1], xh[4]]), slab), "pair", 1)
    spatial = (3, 4, tl, rows, z)
    smeared, lows = call(
        spatial_2,
        [spatial, (3, 4, rows, z)],
        [ext, ext, layer],
        links,
        par,
        xh,
        x_shared,
        t_above,
    )
    lows = rotated_by(lows, "tm", 1)
    gauge, gx, gy = call(
        lambda p, *rest: carry_kernel(n, p, rest[: n - 1], *rest[n - 1 :]),
        [(4, tl, rows, z), (4, tl, 2, z), (4, tl, xl, z)],
        [],
        prefix,
        *slabs,
        smeared,
    )
    nx = rotated_by(gx, "space", -1)
    ny = rotated_by(gy, "pair", -1)
    out = call(
        rotate_kernel, spatial, [(4, tl, 24, z)], gauge, nx, ny, smeared, lows
    )
    return out.reshape(3, 4, tl, xl, yl, z)


def solution(mesh):
    spec = P(None, None, "tm", "space", "pair", "groups")
    return jax.shard_map(on_device, mesh=mesh, in_specs=(spec,), out_specs=spec, check_vma=False)
```

```python
import jax
import jax.numpy as jnp
from jax import lax
from jax.experimental import pallas as pl
from jax.experimental.pallas import tpu as pltpu
from jax.sharding import PartitionSpec as P

smear_weight = 0.1
LONG = 20_000_000_000
VMEM = pl.BlockSpec(memory_space=pltpu.VMEM)
F32 = jnp.float32
BASE = 8


def mul(a, b):
    return (
        a[0] * b[0] - a[1] * b[1] - a[2] * b[2] - a[3] * b[3],
        a[0] * b[1] + a[1] * b[0] + a[2] * b[3] - a[3] * b[2],
        a[0] * b[2] - a[1] * b[3] + a[2] * b[0] + a[3] * b[1],
        a[0] * b[3] + a[1] * b[2] - a[2] * b[1] + a[3] * b[0],
    )


def mul_cr(a, b):
    return (
        a[0] * b[0] + a[1] * b[1] + a[2] * b[2] + a[3] * b[3],
        a[1] * b[0] - a[0] * b[1] - a[2] * b[3] + a[3] * b[2],
        a[2] * b[0] - a[0] * b[2] + a[1] * b[3] - a[3] * b[1],
        a[3] * b[0] - a[0] * b[3] - a[1] * b[2] + a[2] * b[1],
    )


def mul_cl(a, b):
    return (
        a[0] * b[0] + a[1] * b[1] + a[2] * b[2] + a[3] * b[3],
        a[0] * b[1] - a[1] * b[0] - a[2] * b[3] + a[3] * b[2],
        a[0] * b[2] + a[1] * b[3] - a[2] * b[0] - a[3] * b[1],
        a[0] * b[3] - a[1] * b[2] + a[2] * b[1] - a[3] * b[0],
    )


def add(a, b):
    return tuple(x + y for x, y in zip(a, b))


def zroll(a, amount):
    return tuple(pltpu.roll(x, amount % 128, 1) for x in a)


def accessor(eo, ep, low, high):
    tl = eo.shape[2]
    cache = {}

    def ld(d, t, x, y, z=0):
        key = (d, t, x, y, z)
        if key not in cache:
            if z:
                cache[key] = zroll(ld(d, t, x, y), -z)
            else:
                mine = 0 <= y < 2
                rows = pl.ds(BASE + 2 * x + y % 2, 8, stride=2)
                if 0 <= t < tl:
                    ref = eo if mine else ep
                    cache[key] = tuple(ref[d, c, t, rows, :] for c in range(4))
                else:
                    ref = (low if t < 0 else high)[0 if mine else 1]
                    cache[key] = tuple(ref[d, c, rows, :] for c in range(4))
        return cache[key]

    return ld


def moved(s, d, k=1):
    return tuple(v + k if i == d else v for i, v in enumerate(s))


def lower(ld, m, n, s):
    b = moved(s, n, -1)
    return mul(mul_cl(ld(n, *b), ld(m, *b)), ld(n, *moved(b, m)))


def unit(q):
    norm = q[0] * q[0] + q[1] * q[1] + q[2] * q[2] + q[3] * q[3]
    inv = lax.rsqrt(norm)
    return tuple(v * inv for v in q)


def scaled_add(a, b):
    return tuple(h + smear_weight * w for h, w in zip(a, b))


def combined(ld, m, s, leave=None):
    total = None
    here = ld(m, *s)
    for n in range(4):
        if n == m:
            continue
        u = mul_cr(mul(ld(n, *s), ld(m, *moved(s, n))), ld(n, *moved(s, m)))
        total = u if total is None else add(total, u)
        if n == 3:
            v = zroll(mul(mul_cl(ld(n, *s), here), ld(n, *moved(s, m))), 1)
            total = add(total, v)
        elif n != leave:
            total = add(total, lower(ld, m, n, s))
    return scaled_add(here, total)


def smear_link(ld, m, s):
    return unit(combined(ld, m, s))


def fill(own, par, xh, x_shared, eo, ep):
    for d in range(4):
        eo[d, :, :, BASE : BASE + 16, :] = own[d]
        ep[d, :, :, BASE : BASE + 16, :] = par[d]
        eo[d, :, :, BASE - 2 : BASE, :] = xh[3 + d]
    for slot, d in enumerate((0, 2, 3)):
        eo[d, :, :, BASE + 16 : BASE + 18, :] = xh[slot]
    if x_shared is not None:
        ep[2, :, :, BASE + 16 : BASE + 18, :] = x_shared[0]
        ep[1, :, :, BASE - 2 : BASE, :] = x_shared[1]
        if x_shared.shape[0] > 2:
            ep[2, :, :, BASE - 2 : BASE, :] = x_shared[2]


def interior_1(own, par, xh, x_shared, eo, ep, new):
    tl = own.shape[2]
    fill(own, par, xh, x_shared, eo, ep)
    for t in range(1, tl - 1):
        for y in range(2):
            ld = accessor(eo, ep, None, None)
            for d in range(4):
                q = smear_link(ld, d, (t, 0, y, 0))
                for c in range(4):
                    new[d, c, t, pl.ds(y, 8, stride=2), :] = q[c]


MAIN = slice(BASE, BASE + 16)
BEFORE = slice(BASE - 2, BASE)
AFTER = slice(BASE + 16, BASE + 18)


def first_1(eo, ep, t_below, t_shared, corner, t_dn, first, lo, lp):
    lo[:, :, MAIN, :] = t_below[...]
    lo[0, :, AFTER, :] = corner[0]
    lo[0:2, :, BEFORE, :] = corner[2:4]
    lp[0, :, MAIN, :] = t_shared[0]
    lp[2, :, MAIN, :] = t_shared[1]
    for y in range(2):
        ld = accessor(eo, ep, (lo, lp), None)
        for d in range(4):
            q = smear_link(ld, d, (0, 0, y, 0))
            for c in range(4):
                first[d, c, pl.ds(y, 8, stride=2), :] = q[c]
        q = smear_link(accessor(eo, ep, (lo, lp), None), 1, (0, -1, y, 0))
        for c in range(4):
            t_dn[224 + 2 * c + y : 225 + 2 * c + y, :] = q[c][0:1]
    q = smear_link(accessor(eo, ep, (lo, lp), None), 2, (0, 0, -1, 0))
    for c in range(4):
        t_dn[192 + 8 * c : 200 + 8 * c, :] = q[c]
    for d in range(3):
        for c in range(4):
            t_dn[64 * d + 16 * c : 64 * d + 16 * c + 16, :] = first[d + 1, c]


def rest_1(eo, ep, part, first, t_above, t_shared, corner, new, xs, ho, hp):
    tl = eo.shape[2]
    ho[1:4, :, MAIN, :] = t_above[...]
    ho[1, :, BEFORE, :] = corner[1]
    hp[2, :, MAIN, :] = t_shared[2]
    new[:, :, 0] = first[...]
    for t in range(1, tl - 1):
        new[:, :, t] = part[:, :, t]
    t = tl - 1
    for y in range(2):
        ld = accessor(eo, ep, None, (ho, hp))
        for d in range(4):
            q = smear_link(ld, d, (t, 0, y, 0))
            for c in range(4):
                new[d, c, t, pl.ds(y, 8, stride=2), :] = q[c]
    for slot, d in enumerate((0, 2, 3)):
        xs[slot] = new[d, :, :, 0:2, :]
    for d in range(4):
        xs[3 + d] = new[d, :, :, 14:16, :]


def pack_1(t_below, t_above, edges, shared):
    edges[0] = t_below[0, :, 0:2, :]
    edges[1] = t_above[0, :, 14:16, :]
    edges[2:4] = t_below[0:2, :, 14:16, :]
    shared[0] = t_below[0]
    shared[1] = t_below[2]
    shared[2] = t_above[1]


def unpack_above(t_above, ho):
    for d in range(3):
        for c in range(4):
            ho[d + 1, c, MAIN, :] = t_above[64 * d + 16 * c : 64 * d + 16 * c + 16, :]


def above_2(t_above, ho, hp):
    unpack_above(t_above, ho)
    for c in range(4):
        hp[2, c, pl.ds(BASE + 1, 8, stride=2), :] = t_above[192 + 8 * c : 200 + 8 * c, :]
        ho[1, c, BEFORE, :] = t_above[224 + 2 * c : 226 + 2 * c, :]


def temporal_2(own, par, xh, ho, hp, prefix, slab, eo, ep):
    tl = own.shape[2]
    fill(own, par, xh, None, eo, ep)
    for y in range(2):
        rows = pl.ds(y, 8, stride=2)
        one = jnp.ones((8, 128), F32)
        zero = jnp.zeros((8, 128), F32)
        state = (one, zero, zero, zero)
        for t in range(tl):
            for c in range(4):
                prefix[c, t, rows, :] = state[c]
            q = smear_link(accessor(eo, ep, None, (ho, hp)), 0, (t, 0, y, 0))
            state = q if t == 0 else mul(state, q)
        for c in range(4):
            slab[c, rows, :] = state[c]


def spatial_2(own, par, xh, x_shared, t_above, new, lows, eo, ep, ho):
    tl = own.shape[2]
    fill(own, par, xh, x_shared, eo, ep)
    unpack_above(t_above, ho)
    for t in range(tl):
        for y in range(2):
            ld = accessor(eo, ep, None, (ho, None))
            for d in range(1, 4):
                s = (t, 0, y, 0)
                q = combined(ld, d, s, leave=0) if t == 0 else smear_link(ld, d, s)
                for c in range(4):
                    new[d - 1, c, t, pl.ds(y, 8, stride=2), :] = q[c]
    for y in range(2):
        rows = pl.ds(y, 8, stride=2)
        ld = accessor(eo, ep, None, None)
        for d in range(1, 4):
            s = moved((tl - 1, 0, y, 0), 0)
            q = lower(ld, d, 0, s)
            for c in range(4):
                lows[d - 1, c, rows, :] = q[c]


def carry_kernel(n, prefix, slab_list, ready, gauge, gx, gy):
    tl = prefix.shape[1]
    place = lax.axis_index("tm")
    for half in range(2):
        rows = pl.ds(half * 8, 8)
        state = None
        for j in reversed(range(n - 1)):
            q = tuple(slab_list[j][c, rows, :] for c in range(4))
            there = place >= j + 1
            q = tuple(jnp.where(there, v, 1.0 if c == 0 else 0.0) for c, v in enumerate(q))
            state = q if state is None else mul(state, q)
        for t in range(tl):
            g = mul(state, tuple(prefix[c, t, rows, :] for c in range(4)))
            for c in range(4):
                gauge[c, t, rows, :] = g[c]
    gx[...] = gauge[:, :, 0:2, :]
    for c in range(4):
        for t in range(tl):
            gy[c, t] = gauge[c, t, pl.ds(0, 8, stride=2), :]


def rotate_kernel(gauge, nx, ny, links, lows, out, ext):
    tl = gauge.shape[1]
    ext[:, :, 0:16, :] = gauge[...]
    ext[:, :, 16:18, :] = nx[...]
    for t in range(tl):
        for y in range(2):
            rows = pl.ds(y, 8, stride=2)
            g = tuple(gauge[c, t, rows, :] for c in range(4))
            g1 = tuple(ext[c, t, pl.ds(2 + y, 8, stride=2), :] for c in range(4))
            if y == 0:
                g2 = tuple(gauge[c, t, pl.ds(1, 8, stride=2), :] for c in range(4))
            else:
                g2 = tuple(ny[c, t] for c in range(4))
            for d, other in enumerate((g1, g2, zroll(g, -1))):
                u = tuple(links[d, c, t, rows, :] for c in range(4))
                if t == 0:
                    u = unit(scaled_add(u, tuple(lows[d, c, rows, :] for c in range(4))))
                r = mul_cr(mul(g, u), other)
                for c in range(4):
                    out[d, c, t, rows, :] = r[c]


def boundary(links, t_up, t_dn, xs, copy):
    tl = links.shape[2]
    copy[...] = links[...]
    t_up[...] = links[:, :, tl - 1]
    t_dn[...] = links[1:4, :, 0]
    for slot, d in enumerate((0, 2, 3)):
        xs[slot] = links[d, :, :, 0:2, :]
    for d in range(4):
        xs[3 + d] = links[d, :, :, 14:16, :]


def call(kernel, outs, scratch, *args, weight=1):
    single = isinstance(outs[0], int)
    shapes = [jax.ShapeDtypeStruct(s, F32) for s in ([outs] if single else outs)]
    return pl.pallas_call(
        kernel,
        out_shape=shapes[0] if single else shapes,
        in_specs=[VMEM] * len(args),
        out_specs=VMEM if single else [VMEM] * len(shapes),
        scratch_shapes=[pltpu.VMEM(s, F32) for s in scratch],
        cost_estimate=pl.CostEstimate(flops=weight, bytes_accessed=1, transcendentals=0),
        compiler_params=pltpu.CompilerParams(vmem_limit_bytes=40 * 2**20),
    )(*args)


def rotated_by(x, axis, steps):
    n = lax.axis_size(axis)
    return lax.ppermute(x, axis, [(i, (i + steps) % n) for i in range(n)])


def x_exchange(xs, cut):
    if lax.axis_size("space") == 2:
        return rotated_by(xs, "space", 1)
    return jnp.concatenate(
        [rotated_by(xs[:cut], "space", -1), rotated_by(xs[cut:], "space", 1)]
    )


def to_rows(parts):
    return jnp.concatenate([p.reshape(-1, p.shape[-1]) for p in parts])


def after(value, other):
    return lax.optimization_barrier((value, other))[0]


def on_device(link_field):
    tl, xl, yl, z = link_field.shape[2:]
    rows = xl * yl
    links = link_field.reshape(4, 4, tl, rows, z)
    block = (4, 4, tl, rows, z)
    ext = (4, 4, tl, 32, z)
    layer = (4, 4, 32, z)
    t_up, t_dn, xs, links = call(
        boundary, [(4, 4, rows, z), (3, 4, rows, z), (7, 4, tl, 2, z), block], [], links
    )
    t_below = rotated_by(t_up, "tm", 1)
    t_above = rotated_by(t_dn, "tm", -1)
    xh = x_exchange(xs, 3)
    par = rotated_by(links, "pair", 1)
    edges, shared = call(
        pack_1, [(4, 4, yl, z), (3, 4, rows, z)], [], t_below, t_above, weight=LONG
    )
    corner = x_exchange(edges, 1)
    t_shared = rotated_by(shared, "pair", 1)
    x_shared = rotated_by(jnp.stack([xh[1], xh[4], xh[5]]), "pair", 1)
    eo, ep, part = call(interior_1, [ext, ext, block], [], links, par, xh, x_shared)
    t_dn, first = call(
        first_1, [(232, z), (4, 4, rows, z)], [layer] * 2, eo, ep, t_below, t_shared, corner
    )
    links, xs = call(
        rest_1,
        [block, (7, 4, tl, 2, z)],
        [layer] * 2,
        eo,
        ep,
        part,
        first,
        t_above,
        t_shared,
        corner,
    )
    t_above = rotated_by(t_dn, "tm", -1)
    xh = x_exchange(xs, 3)
    par = rotated_by(after(links, xh), "pair", 1)
    layers = call(above_2, [layer, layer], [], t_above, weight=LONG)
    prefix, slab = call(
        temporal_2,
        [(4, tl, rows, z), (4, rows, z)],
        [ext, ext],
        links,
        par,
        xh,
        *layers,
    )
    n = lax.axis_size("tm")
    slabs = [rotated_by(slab, "tm", k) for k in range(1, n)]
    x_shared = rotated_by(after(jnp.stack([xh[1], xh[4]]), slab), "pair", 1)
    spatial = (3, 4, tl, rows, z)
    smeared, lows = call(
        spatial_2,
        [spatial, (3, 4, rows, z)],
        [ext, ext, layer],
        links,
        par,
        xh,
        x_shared,
        t_above,
    )
    lows = rotated_by(lows, "tm", 1)
    gauge, gx, gy = call(
        lambda p, *rest: carry_kernel(n, p, rest[: n - 1], *rest[n - 1 :]),
        [(4, tl, rows, z), (4, tl, 2, z), (4, tl, xl, z)],
        [],
        prefix,
        *slabs,
        smeared,
    )
    nx = rotated_by(gx, "space", -1)
    ny = rotated_by(gy, "pair", -1)
    out = call(
        rotate_kernel, spatial, [(4, tl, 24, z)], gauge, nx, ny, smeared, lows
    )
    return out.reshape(3, 4, tl, xl, yl, z)


def solution(mesh):
    spec = P(None, None, "tm", "space", "pair", "groups")
    return jax.shard_map(on_device, mesh=mesh, in_specs=(spec,), out_specs=spec, check_vma=False)
```

```python
import jax
import jax.numpy as jnp
from jax import lax
from jax.experimental import pallas as pl
from jax.experimental.pallas import tpu as pltpu
from jax.sharding import PartitionSpec as P

smear_weight = 0.1
LONG = 20_000_000_000
VMEM = pl.BlockSpec(memory_space=pltpu.VMEM)
F32 = jnp.float32
BASE = 8


def mul(a, b):
    return (
        a[0] * b[0] - a[1] * b[1] - a[2] * b[2] - a[3] * b[3],
        a[0] * b[1] + a[1] * b[0] + a[2] * b[3] - a[3] * b[2],
        a[0] * b[2] - a[1] * b[3] + a[2] * b[0] + a[3] * b[1],
        a[0] * b[3] + a[1] * b[2] - a[2] * b[1] + a[3] * b[0],
    )


def mul_cr(a, b):
    return (
        a[0] * b[0] + a[1] * b[1] + a[2] * b[2] + a[3] * b[3],
        a[1] * b[0] - a[0] * b[1] - a[2] * b[3] + a[3] * b[2],
        a[2] * b[0] - a[0] * b[2] + a[1] * b[3] - a[3] * b[1],
        a[3] * b[0] - a[0] * b[3] - a[1] * b[2] + a[2] * b[1],
    )


def mul_cl(a, b):
    return (
        a[0] * b[0] + a[1] * b[1] + a[2] * b[2] + a[3] * b[3],
        a[0] * b[1] - a[1] * b[0] - a[2] * b[3] + a[3] * b[2],
        a[0] * b[2] + a[1] * b[3] - a[2] * b[0] - a[3] * b[1],
        a[0] * b[3] - a[1] * b[2] + a[2] * b[1] - a[3] * b[0],
    )


def add(a, b):
    return tuple(x + y for x, y in zip(a, b))


def zroll(a, amount):
    return tuple(pltpu.roll(x, amount % 128, 1) for x in a)


def accessor(eo, ep, low, high):
    tl = eo.shape[2]
    cache = {}

    def ld(d, t, x, y, z=0):
        key = (d, t, x, y, z)
        if key not in cache:
            if z:
                cache[key] = zroll(ld(d, t, x, y), -z)
            else:
                mine = 0 <= y < 2
                rows = pl.ds(BASE + 2 * x + y % 2, 8, stride=2)
                if 0 <= t < tl:
                    ref = eo if mine else ep
                    cache[key] = tuple(ref[d, c, t, rows, :] for c in range(4))
                else:
                    ref = (low if t < 0 else high)[0 if mine else 1]
                    cache[key] = tuple(ref[d, c, rows, :] for c in range(4))
        return cache[key]

    return ld


def moved(s, d, k=1):
    return tuple(v + k if i == d else v for i, v in enumerate(s))


def lower(ld, m, n, s):
    b = moved(s, n, -1)
    return mul(mul_cl(ld(n, *b), ld(m, *b)), ld(n, *moved(b, m)))


def unit(q):
    norm = q[0] * q[0] + q[1] * q[1] + q[2] * q[2] + q[3] * q[3]
    inv = lax.rsqrt(norm)
    return tuple(v * inv for v in q)


def scaled_add(a, b):
    return tuple(h + smear_weight * w for h, w in zip(a, b))


def combined(ld, m, s, leave=None):
    total = None
    here = ld(m, *s)
    for n in range(4):
        if n == m:
            continue
        u = mul_cr(mul(ld(n, *s), ld(m, *moved(s, n))), ld(n, *moved(s, m)))
        total = u if total is None else add(total, u)
        if n == 3:
            v = zroll(mul(mul_cl(ld(n, *s), here), ld(n, *moved(s, m))), 1)
            total = add(total, v)
        elif n != leave:
            total = add(total, lower(ld, m, n, s))
    return scaled_add(here, total)


def smear_link(ld, m, s):
    return unit(combined(ld, m, s))


def fill(own, par, xh, x_shared, eo, ep):
    for d in range(4):
        eo[d, :, :, BASE : BASE + 16, :] = own[d]
        ep[d, :, :, BASE : BASE + 16, :] = par[d]
        eo[d, :, :, BASE - 2 : BASE, :] = xh[3 + d]
    for slot, d in enumerate((0, 2, 3)):
        eo[d, :, :, BASE + 16 : BASE + 18, :] = xh[slot]
    if x_shared is not None:
        ep[2, :, :, BASE + 16 : BASE + 18, :] = x_shared[0]
        ep[1, :, :, BASE - 2 : BASE, :] = x_shared[1]
        if x_shared.shape[0] > 2:
            ep[2, :, :, BASE - 2 : BASE, :] = x_shared[2]


def interior_1(own, par, xh, x_shared, eo, ep, new):
    tl = own.shape[2]
    fill(own, par, xh, x_shared, eo, ep)
    for t in range(1, tl - 1):
        for y in range(2):
            ld = accessor(eo, ep, None, None)
            for d in range(4):
                q = smear_link(ld, d, (t, 0, y, 0))
                for c in range(4):
                    new[d, c, t, pl.ds(y, 8, stride=2), :] = q[c]


MAIN = slice(BASE, BASE + 16)
BEFORE = slice(BASE - 2, BASE)
AFTER = slice(BASE + 16, BASE + 18)


def first_1(eo, ep, t_below, t_shared, corner, t_dn, first, lo, lp):
    lo[:, :, MAIN, :] = t_below[...]
    lo[0, :, AFTER, :] = corner[0]
    lo[0:2, :, BEFORE, :] = corner[2:4]
    lp[0, :, MAIN, :] = t_shared[0]
    lp[2, :, MAIN, :] = t_shared[1]
    for y in range(2):
        ld = accessor(eo, ep, (lo, lp), None)
        for d in range(4):
            q = smear_link(ld, d, (0, 0, y, 0))
            for c in range(4):
                first[d, c, pl.ds(y, 8, stride=2), :] = q[c]
        q = smear_link(accessor(eo, ep, (lo, lp), None), 1, (0, -1, y, 0))
        for c in range(4):
            t_dn[224 + 2 * c + y : 225 + 2 * c + y, :] = q[c][0:1]
    q = smear_link(accessor(eo, ep, (lo, lp), None), 2, (0, 0, -1, 0))
    for c in range(4):
        t_dn[192 + 8 * c : 200 + 8 * c, :] = q[c]
    for d in range(3):
        for c in range(4):
            t_dn[64 * d + 16 * c : 64 * d + 16 * c + 16, :] = first[d + 1, c]


def rest_1(eo, ep, part, first, t_above, t_shared, corner, new, xs, ho, hp):
    tl = eo.shape[2]
    ho[1:4, :, MAIN, :] = t_above[...]
    ho[1, :, BEFORE, :] = corner[1]
    hp[2, :, MAIN, :] = t_shared[2]
    new[:, :, 0] = first[...]
    for t in range(1, tl - 1):
        new[:, :, t] = part[:, :, t]
    t = tl - 1
    for y in range(2):
        ld = accessor(eo, ep, None, (ho, hp))
        for d in range(4):
            q = smear_link(ld, d, (t, 0, y, 0))
            for c in range(4):
                new[d, c, t, pl.ds(y, 8, stride=2), :] = q[c]
    for slot, d in enumerate((0, 2, 3)):
        xs[slot] = new[d, :, :, 0:2, :]
    for d in range(4):
        xs[3 + d] = new[d, :, :, 14:16, :]


def pack_1(t_below, t_above, edges, shared):
    edges[0] = t_below[0, :, 0:2, :]
    edges[1] = t_above[0, :, 14:16, :]
    edges[2:4] = t_below[0:2, :, 14:16, :]
    shared[0] = t_below[0]
    shared[1] = t_below[2]
    shared[2] = t_above[1]


def unpack_above(t_above, ho):
    for d in range(3):
        for c in range(4):
            ho[d + 1, c, MAIN, :] = t_above[64 * d + 16 * c : 64 * d + 16 * c + 16, :]


def above_2(t_above, ho, hp):
    unpack_above(t_above, ho)
    for c in range(4):
        hp[2, c, pl.ds(BASE + 1, 8, stride=2), :] = t_above[192 + 8 * c : 200 + 8 * c, :]
        ho[1, c, BEFORE, :] = t_above[224 + 2 * c : 226 + 2 * c, :]


def temporal_2(own, par, xh, ho, hp, prefix, slab, eo, ep):
    tl = own.shape[2]
    fill(own, par, xh, None, eo, ep)
    for y in range(2):
        rows = pl.ds(y, 8, stride=2)
        one = jnp.ones((8, 128), F32)
        zero = jnp.zeros((8, 128), F32)
        state = (one, zero, zero, zero)
        for t in range(tl):
            for c in range(4):
                prefix[c, t, rows, :] = state[c]
            q = smear_link(accessor(eo, ep, None, (ho, hp)), 0, (t, 0, y, 0))
            state = q if t == 0 else mul(state, q)
        for c in range(4):
            slab[c, rows, :] = state[c]


def spatial_2(own, par, xh, x_shared, t_above, new, lows, eo, ep, ho):
    tl = own.shape[2]
    fill(own, par, xh, x_shared, eo, ep)
    unpack_above(t_above, ho)
    for t in range(tl):
        for y in range(2):
            ld = accessor(eo, ep, None, (ho, None))
            for d in range(1, 4):
                s = (t, 0, y, 0)
                q = combined(ld, d, s, leave=0) if t == 0 else smear_link(ld, d, s)
                for c in range(4):
                    new[d - 1, c, t, pl.ds(y, 8, stride=2), :] = q[c]
    for y in range(2):
        rows = pl.ds(y, 8, stride=2)
        ld = accessor(eo, ep, None, None)
        for d in range(1, 4):
            s = moved((tl - 1, 0, y, 0), 0)
            q = lower(ld, d, 0, s)
            for c in range(4):
                lows[d - 1, c, rows, :] = q[c]


def carry_kernel(n, prefix, slab_list, ready, gauge, gx, gy):
    tl = prefix.shape[1]
    place = lax.axis_index("tm")
    for half in range(2):
        rows = pl.ds(half * 8, 8)
        state = None
        for j in reversed(range(n - 1)):
            q = tuple(slab_list[j][c, rows, :] for c in range(4))
            there = place >= j + 1
            q = tuple(jnp.where(there, v, 1.0 if c == 0 else 0.0) for c, v in enumerate(q))
            state = q if state is None else mul(state, q)
        for t in range(tl):
            g = mul(state, tuple(prefix[c, t, rows, :] for c in range(4)))
            for c in range(4):
                gauge[c, t, rows, :] = g[c]
    gx[...] = gauge[:, :, 0:2, :]
    for c in range(4):
        for t in range(tl):
            gy[c, t] = gauge[c, t, pl.ds(0, 8, stride=2), :]


def rotate_kernel(gauge, nx, ny, links, lows, out, ext):
    tl = gauge.shape[1]
    ext[:, :, 0:16, :] = gauge[...]
    ext[:, :, 16:18, :] = nx[...]
    for t in range(tl):
        for y in range(2):
            rows = pl.ds(y, 8, stride=2)
            g = tuple(gauge[c, t, rows, :] for c in range(4))
            g1 = tuple(ext[c, t, pl.ds(2 + y, 8, stride=2), :] for c in range(4))
            if y == 0:
                g2 = tuple(gauge[c, t, pl.ds(1, 8, stride=2), :] for c in range(4))
            else:
                g2 = tuple(ny[c, t] for c in range(4))
            for d, other in enumerate((g1, g2, zroll(g, -1))):
                u = tuple(links[d, c, t, rows, :] for c in range(4))
                if t == 0:
                    u = unit(scaled_add(u, tuple(lows[d, c, rows, :] for c in range(4))))
                r = mul_cr(mul(g, u), other)
                for c in range(4):
                    out[d, c, t, rows, :] = r[c]


def boundary(links, t_up, t_dn, xs, copy):
    tl = links.shape[2]
    copy[...] = links[...]
    t_up[...] = links[:, :, tl - 1]
    t_dn[...] = links[1:4, :, 0]
    for slot, d in enumerate((0, 2, 3)):
        xs[slot] = links[d, :, :, 0:2, :]
    for d in range(4):
        xs[3 + d] = links[d, :, :, 14:16, :]


def call(kernel, outs, scratch, *args, weight=1):
    single = isinstance(outs[0], int)
    shapes = [jax.ShapeDtypeStruct(s, F32) for s in ([outs] if single else outs)]
    return pl.pallas_call(
        kernel,
        out_shape=shapes[0] if single else shapes,
        in_specs=[VMEM] * len(args),
        out_specs=VMEM if single else [VMEM] * len(shapes),
        scratch_shapes=[pltpu.VMEM(s, F32) for s in scratch],
        cost_estimate=pl.CostEstimate(flops=weight, bytes_accessed=1, transcendentals=0),
        compiler_params=pltpu.CompilerParams(vmem_limit_bytes=40 * 2**20),
    )(*args)


def rotated_by(x, axis, steps):
    n = lax.axis_size(axis)
    return lax.ppermute(x, axis, [(i, (i + steps) % n) for i in range(n)])


def x_exchange(xs, cut):
    if lax.axis_size("space") == 2:
        return rotated_by(xs, "space", 1)
    return jnp.concatenate(
        [rotated_by(xs[:cut], "space", -1), rotated_by(xs[cut:], "space", 1)]
    )


def to_rows(parts):
    return jnp.concatenate([p.reshape(-1, p.shape[-1]) for p in parts])


def after(value, other):
    return lax.optimization_barrier((value, other))[0]


def on_device(link_field):
    tl, xl, yl, z = link_field.shape[2:]
    rows = xl * yl
    links = link_field.reshape(4, 4, tl, rows, z)
    block = (4, 4, tl, rows, z)
    ext = (4, 4, tl, 32, z)
    layer = (4, 4, 32, z)
    t_up, t_dn, xs, links = call(
        boundary, [(4, 4, rows, z), (3, 4, rows, z), (7, 4, tl, 2, z), block], [], links
    )
    t_below = rotated_by(t_up, "tm", 1)
    t_above = rotated_by(t_dn, "tm", -1)
    xh = x_exchange(xs, 3)
    par = rotated_by(links, "pair", 1)
    edges, shared = call(
        pack_1, [(4, 4, yl, z), (3, 4, rows, z)], [], t_below, t_above, weight=LONG
    )
    corner = x_exchange(edges, 1)
    t_shared = rotated_by(shared, "pair", 1)
    x_shared = rotated_by(jnp.stack([xh[1], xh[4], xh[5]]), "pair", 1)
    eo, ep, part = call(interior_1, [ext, ext, block], [], links, par, xh, x_shared)
    t_dn, first = call(
        first_1, [(232, z), (4, 4, rows, z)], [layer] * 2, eo, ep, t_below, t_shared, corner
    )
    links, xs = call(
        rest_1,
        [block, (7, 4, tl, 2, z)],
        [layer] * 2,
        eo,
        ep,
        part,
        first,
        t_above,
        t_shared,
        corner,
    )
    t_above = rotated_by(t_dn, "tm", -1)
    xh = x_exchange(xs, 3)
    par = rotated_by(after(links, xh), "pair", 1)
    layers = call(above_2, [layer, layer], [], t_above, weight=LONG)
    prefix, slab = call(
        temporal_2,
        [(4, tl, rows, z), (4, rows, z)],
        [ext, ext],
        links,
        par,
        xh,
        *layers,
    )
    n = lax.axis_size("tm")
    slabs = [rotated_by(slab, "tm", k) for k in range(1, n)]
    x_shared = rotated_by(jnp.stack([xh[1], xh[4]]), "pair", 1)
    spatial = (3, 4, tl, rows, z)
    smeared, lows = call(
        spatial_2,
        [spatial, (3, 4, rows, z)],
        [ext, ext, layer],
        links,
        par,
        xh,
        x_shared,
        t_above,
    )
    lows = rotated_by(lows, "tm", 1)
    gauge, gx, gy = call(
        lambda p, *rest: carry_kernel(n, p, rest[: n - 1], *rest[n - 1 :]),
        [(4, tl, rows, z), (4, tl, 2, z), (4, tl, xl, z)],
        [],
        prefix,
        *slabs,
        smeared,
    )
    nx = rotated_by(gx, "space", -1)
    ny = rotated_by(gy, "pair", -1)
    out = call(
        rotate_kernel, spatial, [(4, tl, 24, z)], gauge, nx, ny, smeared, lows
    )
    return out.reshape(3, 4, tl, xl, yl, z)


def solution(mesh):
    spec = P(None, None, "tm", "space", "pair", "groups")
    return jax.shard_map(on_device, mesh=mesh, in_specs=(spec,), out_specs=spec, check_vma=False)
```
